32 devices in a mesh: dp: 16 (over z, x, core), tensor: 2 (over y).
Axes of the slice: x: 2, y: 2, z: 4, core: 2. Of those that a mesh axis runs over, the one named last changes fastest.
Arguments:
- inputs: bfloat16 [3152, 768], P('dp'), may hold values from -6 to 6
- cotangent: bfloat16 [3152, 768], P('dp'), may hold values from -6 to 6
- mixing_weight: bfloat16 [3, 768, 768], P(None, 'dp', 'tensor'), may hold values from -0.21875 to 0.21875
- output_weight: bfloat16 [768, 768], P('tensor', 'dp'), may hold values from -0.875 to 0.875
- up_weight: bfloat16 [768, 3072], P('dp', 'tensor'), may hold values from -0.21875 to 0.21875
- down_weight: bfloat16 [3072, 768], P('tensor', 'dp'), may hold values from -0.109375 to 0.109375
- first_gain: float32 [768], replicated, may hold values from 0.5 to 1.5
- first_shift: float32 [768], replicated, may hold values from -3 to 3
- attend_bias: float32 [2, 768], P(None, 'tensor'), may hold values from -3 to 3
- output_bias: float32 [768], replicated, may hold values from -3 to 3
- hidden_bias: float32 [3072], P('tensor'), may hold values from -3 to 3
- final_bias: float32 [768], replicated, may hold values from -3 to 3
- second_gain: float32 [768], replicated, may hold values from 0.5 to 1.5
- second_shift: float32 [768], replicated, may hold values from -3 to 3
Outputs:
- layer_output: bfloat16 [3152, 768], P('dp')
- input_grad: bfloat16 [3152, 768], P('dp')
- mixing_grad: float32 [3, 768, 768], P(None, 'dp', 'tensor')
- outweight_grad: float32 [768, 768], P('tensor', 'dp')
- upweight_grad: float32 [768, 3072], P('dp', 'tensor')
- downweight_grad: float32 [3072, 768], P('tensor', 'dp')
- firstgain_grad: float32 [768], replicated
- firstshift_grad: float32 [768], replicated
- attendbias_grad: float32 [2, 768], P(None, 'tensor')
- outbias_grad: float32 [768], replicated
- hiddenbias_grad: float32 [3072], P('tensor')
- finalbias_grad: float32 [768], replicated
- secondgain_grad: float32 [768], replicated
- secondshift_grad: float32 [768], replicated
The draws below stay inside these ranges and needn't reach their ends.
All inputs are finite; a program needn't handle non-finite values.
Results may differ from the reference program's by a relative error of at most 0.011.
Values may be sent and summed in bfloat16 or wider, within the bound.
A program may use at most 128 MiB of HBM per device.

```python
import jax
import jax.numpy as jnp
from jax import lax

D = 768
HD = 64
FF = 3072
SEQ = 197
IMG_DEV = 1
TOKENS = 3152


def strengthened(result, stream_key, source, target, shards_of, factor):
    owner, partner = [(jnp.arange(result.shape[dim]) // (result.shape[dim] // shards_of)).reshape([-1 if axis == dim else 1 for axis in range(result.ndim)]) for dim in (source, target)]
    chosen = jax.random.permutation(stream_key, shards_of)[partner]
    strong = (owner == chosen) | (owner == (partner + shards_of // 2) % shards_of)
    return jnp.where(strong, factor * result, result)


def levels(stream_key, dims, pieces, smallest, largest):
    def one(position, blocks):
        heights = jax.random.uniform(jax.random.fold_in(jax.random.fold_in(stream_key, 6), position), (blocks,), jnp.float32, smallest / len(pieces), largest / len(pieces))
        return jnp.repeat(jnp.exp(heights), dims[position] // blocks).reshape((-1,) + (1,) * (len(dims) - position - 1))

    level = one(*pieces[0])
    for cut in pieces[1:]:
        level = level * one(*cut)
    return level


def centred(key, shape, scale, most, pieces=(), held_as=jnp.bfloat16):
    values = jax.random.normal(key, shape, jnp.float32) * scale
    if len(pieces) > 0:
        values = levels(key, shape, pieces, -0.22, 0.18) * values
    return jnp.clip(values, min=-most, max=most).astype(held_as)


def noise_with(rng, shape, spread, bound, shards, heavy, dtype=jnp.bfloat16):
    array = spread * jax.random.normal(rng, shape, jnp.float32)
    if shards:
        array = array * levels(rng, shape, shards, -0.22, 0.18)
    return jnp.clip(strengthened(array, jax.random.fold_in(rng, 3), *heavy), -bound, bound).astype(dtype)


def setup_inputs(seed: int = 0) -> dict:
    seeds = jax.random.split(jax.random.key(seed), 15)
    inputs = centred(seeds[0], (TOKENS, D), 1.0, 6.0, ((0, 16),))
    cotangent = noise_with(seeds[1], (TOKENS, D), 1.0, 6.0, ((0, 16),), (0, 1, 16, 2.0))
    mixing_weight = centred(seeds[2], (3, D, D), D ** -0.5, 0.21875, ((1, 16), (2, 2)))
    output_weight = centred(seeds[3], (D, D), (D // 16) ** -0.5, 0.875, ((0, 2), (1, 16)))
    up_weight = centred(seeds[4], (D, FF), D ** -0.5, 0.21875, ((0, 16), (1, 2)))
    down_weight = centred(seeds[5], (FF, D), FF ** -0.5, 0.109375, ((0, 2), (1, 16)))
    first_gain = jnp.clip(1.0 + 0.1 * jax.random.normal(seeds[6], (D,), jnp.float32), 0.5, 1.5)
    first_shift = centred(seeds[7], (D,), 0.5, 3.0, (), jnp.float32)
    attend_bias = centred(seeds[8], (2, D), 0.5, 3.0, ((1, 2),), jnp.float32)
    output_bias = centred(seeds[9], (D,), 0.5, 3.0, (), jnp.float32)
    hidden_bias = centred(seeds[10], (FF,), 0.5, 3.0, ((0, 2),), jnp.float32)
    final_bias = centred(seeds[11], (D,), 0.5, 3.0, (), jnp.float32)
    second_gain = jnp.clip(1.0 + 0.1 * jax.random.normal(seeds[12], (D,), jnp.float32), 0.5, 1.5)
    second_shift = centred(seeds[13], (D,), 0.5, 3.0, (), jnp.float32)
    return dict(inputs=inputs, cotangent=cotangent, mixing_weight=mixing_weight, output_weight=output_weight, up_weight=up_weight, down_weight=down_weight, first_gain=first_gain, first_shift=first_shift, attend_bias=attend_bias, output_bias=output_bias, hidden_bias=hidden_bias, final_bias=final_bias, second_gain=second_gain, second_shift=second_shift)


EPSILON = 1e-06

def norm_forward(values, gain, shift):
    center = values - lax.optimization_barrier(jnp.mean(values, axis=-1, keepdims=True))
    inverse = lax.rsqrt(lax.optimization_barrier(jnp.mean(center * center, axis=-1, keepdims=True)) + EPSILON)
    normed = center * inverse
    return (normed, inverse, normed * gain + shift)

def norm_backward(upstream, normed, inverse, gain):
    scaled = upstream * gain
    return inverse * (scaled - lax.optimization_barrier(jnp.mean(scaled, axis=-1, keepdims=True)) - normed * lax.optimization_barrier(jnp.mean(scaled * normed, axis=-1, keepdims=True)))

def gelu_pair(values):
    normal_cdf = 0.5 * (1.0 + lax.erf(values * 0.7071067811865476))
    density = 0.3989422804014327 * jnp.exp(-0.5 * values * values)
    return (values * normal_cdf, normal_cdf + values * density)

def matmul(left, right):
    return jnp.dot(left, right, preferred_element_type=jnp.float32)

def layer(inputs, cotangent, mixing_weight, output_weight, up_weight, down_weight, first_gain, first_shift, attend_bias, output_bias, hidden_bias, final_bias, second_gain, second_shift):
    row_count = inputs.shape[0]
    images = row_count // SEQ
    width = mixing_weight.shape[2]
    split_shape = (images, SEQ, width // HD, HD)
    scale = HD ** (-0.5)
    source = inputs.astype(jnp.float32)
    normed_one, inverse_one, affine_one = norm_forward(source, first_gain, first_shift)
    mixed_in = affine_one.astype(jnp.bfloat16)
    projected = jnp.einsum('nd,jde->jne', mixed_in.astype(jnp.float32), mixing_weight.astype(jnp.float32))
    query = (projected[0] + attend_bias[0]).astype(jnp.bfloat16).reshape(split_shape)
    keys = projected[1].astype(jnp.bfloat16).reshape(split_shape)
    values = (projected[2] + attend_bias[1]).astype(jnp.bfloat16).reshape(split_shape)
    scores = jnp.einsum('bqhd,bkhd->bhqk', query.astype(jnp.float32), keys.astype(jnp.float32)) * scale
    top = lax.optimization_barrier(jnp.max(scores, axis=-1, keepdims=True))
    logsum = top + jnp.log(lax.optimization_barrier(jnp.sum(jnp.exp(scores - top), axis=-1, keepdims=True)))
    probs_full = jnp.exp(scores - logsum)
    probs = probs_full.astype(jnp.bfloat16)
    attended = jnp.einsum('bhqk,bkhd->bqhd', probs.astype(jnp.float32), values.astype(jnp.float32)).astype(jnp.bfloat16).reshape(row_count, width)
    residual = source + matmul(attended, output_weight) + output_bias
    normed_two, inverse_two, affine_two = norm_forward(residual, second_gain, second_shift)
    hidden_in = affine_two.astype(jnp.bfloat16)
    preact = matmul(hidden_in, up_weight) + hidden_bias
    active_full, slope = gelu_pair(preact)
    active = active_full.astype(jnp.bfloat16)
    layer_output = (residual + matmul(active, down_weight) + final_bias).astype(jnp.bfloat16)
    upstream = cotangent.astype(jnp.float32)
    down_grad = matmul(active.T, cotangent)
    finalbias_grad = lax.optimization_barrier(jnp.sum(upstream, axis=0))
    pre_grad = matmul(cotangent, down_weight.T) * slope
    pre_half = pre_grad.astype(jnp.bfloat16)
    up_grad = matmul(hidden_in.T, pre_half)
    hiddenbias_grad = lax.optimization_barrier(jnp.sum(pre_grad, axis=0))
    affine_two_grad = matmul(pre_half, up_weight.T)
    secondgain_grad = lax.optimization_barrier(jnp.sum(affine_two_grad * normed_two, axis=0))
    secondshift_grad = lax.optimization_barrier(jnp.sum(affine_two_grad, axis=0))
    residual_grad = upstream + norm_backward(affine_two_grad, normed_two, inverse_two, second_gain)
    residual_half = residual_grad.astype(jnp.bfloat16)
    outweight_grad = matmul(attended.T, residual_half)
    outbias_grad = lax.optimization_barrier(jnp.sum(residual_grad, axis=0))
    attended_grad = matmul(residual_half, output_weight.T).astype(jnp.bfloat16).reshape(split_shape)
    prob_grad = jnp.einsum('bqhd,bkhd->bhqk', attended_grad.astype(jnp.float32), values.astype(jnp.float32))
    delta = lax.optimization_barrier(jnp.sum(probs_full * prob_grad, axis=-1, keepdims=True))
    score_grad = (probs_full * (prob_grad - delta) * scale).astype(jnp.bfloat16).astype(jnp.float32)
    query_grad = jnp.einsum('bhqk,bkhd->bqhd', score_grad, keys.astype(jnp.float32)).reshape(row_count, width)
    keys_grad = jnp.einsum('bhqk,bqhd->bkhd', score_grad, query.astype(jnp.float32)).reshape(row_count, width)
    values_grad = jnp.einsum('bhqk,bqhd->bkhd', probs.astype(jnp.float32), attended_grad.astype(jnp.float32)).reshape(row_count, width)
    attendbias_grad = jnp.stack([lax.optimization_barrier(jnp.sum(query_grad, axis=0)), lax.optimization_barrier(jnp.sum(values_grad, axis=0))])
    stacked = jnp.stack([query_grad, keys_grad, values_grad]).astype(jnp.bfloat16).astype(jnp.float32)
    mixing_grad = jnp.einsum('nd,jne->jde', mixed_in.astype(jnp.float32), stacked)
    affine_one_grad = jnp.einsum('jne,jde->nd', stacked, mixing_weight.astype(jnp.float32))
    firstgain_grad = lax.optimization_barrier(jnp.sum(affine_one_grad * normed_one, axis=0))
    firstshift_grad = lax.optimization_barrier(jnp.sum(affine_one_grad, axis=0))
    input_grad = (residual_grad + norm_backward(affine_one_grad, normed_one, inverse_one, first_gain)).astype(jnp.bfloat16)
    grads = (mixing_grad, outweight_grad, up_grad, down_grad, firstgain_grad, firstshift_grad, attendbias_grad, outbias_grad, hiddenbias_grad, finalbias_grad, secondgain_grad, secondshift_grad)
    return (layer_output, input_grad, grads)

def reference(inputs, cotangent, mixing_weight, output_weight, up_weight, down_weight, first_gain, first_shift, attend_bias, output_bias, hidden_bias, final_bias, second_gain, second_shift):
    group_rows = IMG_DEV * SEQ
    groups = inputs.shape[0] // group_rows
    params = (mixing_weight, output_weight, up_weight, down_weight, first_gain, first_shift, attend_bias, output_bias, hidden_bias, final_bias, second_gain, second_shift)

    def step(carry, pair):
        output_rows, grad_rows, grads = layer(pair[0], pair[1], *params)
        return (tuple((total + term for total, term in zip(carry, grads))), (output_rows, grad_rows))
    start = tuple((jnp.zeros(param.shape, jnp.float32) for param in params))
    totals, (outputs, in_grads) = lax.scan(step, start, (inputs.reshape(groups, group_rows, D), cotangent.reshape(groups, group_rows, D)))
    return (outputs.reshape(TOKENS, D), in_grads.reshape(TOKENS, D), totals[0], totals[1], totals[2], totals[3], totals[4], totals[5], totals[6], totals[7], totals[8], totals[9], totals[10], totals[11])
```

```python
import functools

import jax
import jax.numpy as jnp
from jax import lax
from jax.experimental import pallas as pl
from jax.experimental.pallas import tpu as pltpu
from jax.sharding import PartitionSpec as P

HD = 64
SEQ = 197


EPSILON = 1e-06


def norm_forward(values, gain, shift):
    center = values - jnp.mean(values, axis=-1, keepdims=True)
    inverse = lax.rsqrt(jnp.mean(center * center, axis=-1, keepdims=True) + EPSILON)
    normed = center * inverse
    return (normed, inverse, normed * gain + shift)


def norm_backward(upstream, normed, inverse, gain):
    scaled = upstream * gain
    return inverse * (
        scaled
        - jnp.mean(scaled, axis=-1, keepdims=True)
        - normed * jnp.mean(scaled * normed, axis=-1, keepdims=True)
    )


def gelu_pair(values):
    normal_cdf = 0.5 * (1.0 + lax.erf(values * 0.7071067811865476))
    density = 0.3989422804014327 * jnp.exp(-0.5 * values * values)
    return (values * normal_cdf, normal_cdf + values * density)


def matmul(left, right):
    return jnp.dot(left, right, preferred_element_type=jnp.float32)


def local_plain(
    inputs,
    cotangent,
    mixing_weight,
    output_weight,
    up_weight,
    down_weight,
    first_gain,
    first_shift,
    attend_bias,
    output_bias,
    hidden_bias,
    final_bias,
    second_gain,
    second_shift,
):
    mixing_full, output_full, up_full, down_full = (
        lax.all_gather(mixing_weight, "dp", axis=1, tiled=True),
        lax.all_gather(output_weight, "dp", axis=1, tiled=True),
        lax.all_gather(up_weight, "dp", axis=0, tiled=True),
        lax.all_gather(down_weight, "dp", axis=1, tiled=True),
    )
    row_count = inputs.shape[0]
    images = row_count // SEQ
    width = mixing_full.shape[2]
    split_shape = (images, SEQ, width // HD, HD)
    scale = HD ** (-0.5)
    source = inputs.astype(jnp.float32)
    normed_one, inverse_one, affine_one = norm_forward(source, first_gain, first_shift)
    mixed_in = affine_one.astype(jnp.bfloat16)
    projected = jnp.einsum("nd,jde->jne", mixed_in, mixing_full, preferred_element_type=jnp.float32)
    query = (projected[0] + attend_bias[0]).astype(jnp.bfloat16).reshape(split_shape)
    keys = projected[1].astype(jnp.bfloat16).reshape(split_shape)
    values = (projected[2] + attend_bias[1]).astype(jnp.bfloat16).reshape(split_shape)
    scores = jnp.einsum("bqhd,bkhd->bhqk", query, keys, preferred_element_type=jnp.float32) * scale
    top = jnp.max(scores, axis=-1, keepdims=True)
    logsum = top + jnp.log(jnp.sum(jnp.exp(scores - top), axis=-1, keepdims=True))
    probs = jnp.exp(scores - logsum).astype(jnp.bfloat16)
    attended = (
        jnp.einsum("bhqk,bkhd->bqhd", probs, values, preferred_element_type=jnp.float32)
        .astype(jnp.bfloat16)
        .reshape(row_count, width)
    )
    residual = source + lax.psum(matmul(attended, output_full), "tensor") + output_bias
    normed_two, inverse_two, affine_two = norm_forward(residual, second_gain, second_shift)
    hidden_in = affine_two.astype(jnp.bfloat16)
    preact = matmul(hidden_in, up_full) + hidden_bias
    active_full, slope = gelu_pair(preact)
    active = active_full.astype(jnp.bfloat16)
    layer_output = (residual + lax.psum(matmul(active, down_full), "tensor") + final_bias).astype(
        jnp.bfloat16
    )
    mixing_back, output_back, up_back, down_back = (mixing_full, output_full, up_full, down_full)
    upstream = cotangent.astype(jnp.float32)
    down_grad = matmul(active.T, cotangent)
    finalbias_grad = jnp.sum(upstream, axis=0)
    pre_grad = matmul(cotangent, down_back.T) * slope
    pre_half = pre_grad.astype(jnp.bfloat16)
    up_grad = matmul(hidden_in.T, pre_half)
    hiddenbias_grad = jnp.sum(pre_grad, axis=0)
    affine_two_grad = lax.psum(matmul(pre_half, up_back.T), "tensor")
    secondgain_grad = jnp.sum(affine_two_grad * normed_two, axis=0)
    secondshift_grad = jnp.sum(affine_two_grad, axis=0)
    residual_grad = upstream + norm_backward(affine_two_grad, normed_two, inverse_two, second_gain)
    residual_half = residual_grad.astype(jnp.bfloat16)
    outweight_grad = matmul(attended.T, residual_half)
    outbias_grad = jnp.sum(residual_grad, axis=0)
    attended_grad = matmul(residual_half, output_back.T).astype(jnp.bfloat16).reshape(split_shape)
    recomputed = (
        jnp.einsum("bqhd,bkhd->bhqk", query, keys, preferred_element_type=jnp.float32) * scale
    )
    probs_full = jnp.exp(recomputed - logsum)
    prob_grad = jnp.einsum(
        "bqhd,bkhd->bhqk", attended_grad, values, preferred_element_type=jnp.float32
    )
    delta = jnp.sum(probs_full * prob_grad, axis=-1, keepdims=True)
    score_grad = (probs_full * (prob_grad - delta) * scale).astype(jnp.bfloat16)
    query_grad = jnp.einsum(
        "bhqk,bkhd->bqhd", score_grad, keys, preferred_element_type=jnp.float32
    ).reshape(row_count, width)
    keys_grad = jnp.einsum(
        "bhqk,bqhd->bkhd", score_grad, query, preferred_element_type=jnp.float32
    ).reshape(row_count, width)
    values_grad = jnp.einsum(
        "bhqk,bqhd->bkhd", probs, attended_grad, preferred_element_type=jnp.float32
    ).reshape(row_count, width)
    attendbias_grad = jnp.stack([jnp.sum(query_grad, axis=0), jnp.sum(values_grad, axis=0)])
    stacked = jnp.stack([query_grad, keys_grad, values_grad]).astype(jnp.bfloat16)
    mixing_grad = jnp.einsum("nd,jne->jde", mixed_in, stacked, preferred_element_type=jnp.float32)
    affine_one_grad = lax.psum(
        jnp.einsum("jne,jde->nd", stacked, mixing_back, preferred_element_type=jnp.float32),
        "tensor",
    )
    firstgain_grad = jnp.sum(affine_one_grad * normed_one, axis=0)
    firstshift_grad = jnp.sum(affine_one_grad, axis=0)
    input_grad = (
        residual_grad + norm_backward(affine_one_grad, normed_one, inverse_one, first_gain)
    ).astype(jnp.bfloat16)
    mixing_share, output_share, up_share, down_share = (
        lax.psum_scatter(mixing_grad, "dp", scatter_dimension=1, tiled=True),
        lax.psum_scatter(outweight_grad, "dp", scatter_dimension=1, tiled=True),
        lax.psum_scatter(up_grad, "dp", scatter_dimension=0, tiled=True),
        lax.psum_scatter(down_grad, "dp", scatter_dimension=1, tiled=True),
    )
    vector_totals = lax.psum(
        (
            firstgain_grad,
            firstshift_grad,
            attendbias_grad,
            outbias_grad,
            hiddenbias_grad,
            finalbias_grad,
            secondgain_grad,
            secondshift_grad,
        ),
        "dp",
    )
    return (
        layer_output,
        input_grad,
        mixing_share,
        output_share,
        up_share,
        down_share,
        vector_totals[0],
        vector_totals[1],
        vector_totals[2],
        vector_totals[3],
        vector_totals[4],
        vector_totals[5],
        vector_totals[6],
        vector_totals[7],
    )


ROWS = 256
SENT = 208
X = 2
C = 2
TILE = 384
SCALE = HD ** (-0.5)
F32 = jnp.float32
BF16 = jnp.bfloat16


def nt(left, right):
    return lax.dot_general(left, right, (((1,), (1,)), ((), ())), preferred_element_type=F32)


def tn(left, right):
    return lax.dot_general(left, right, (((0,), (0,)), ((), ())), preferred_element_type=F32)


def cols(tile):
    return pl.ds(pl.multiple_of(tile * TILE, TILE), TILE)


def layer_kernel(
    Z,
    copies,
    x_ref,
    ct_ref,
    mix_ref,
    outw_ref,
    up_ref,
    down_ref,
    fg_ref,
    fs_ref,
    ab_ref,
    ob_ref,
    hb_ref,
    fb_ref,
    sg_ref,
    ss_ref,
    lo_ref,
    ig_ref,
    gmix_ref,
    gout_ref,
    gup_ref,
    gdown_ref,
    vec_ref,
    w0,
    w1,
    w2,
    w3,
    g0,
    g1,
    g2,
    g3,
    ga0,
    ga1,
    ga2,
    ga3,
    gb0,
    gb1,
    gb2,
    gb3,
    gc0,
    gc1,
    gc2,
    gc3,
    gd0,
    gd1,
    gd2,
    gd3,
    ge0,
    ge1,
    ge2,
    ge3,
    ysend,
    yrecv,
    vs,
    vr,
    left_t,
    n1_s,
    n2_s,
    acc,
    qkv,
    prob_s,
    att,
    attg,
    stacked,
    active,
    slope,
    pre_half,
    a2_s,
    res_s,
    rg_s,
    send_sem,
    recv_sem,
):
    dp = lax.axis_index("dp")
    tensor = lax.axis_index("tensor")
    c = lax.rem(dp, C)
    x = lax.rem(dp // C, X)
    z = dp // (C * X)
    w = (w0, w1, w2, w3)
    g = (g0, g1, g2, g3)
    ga = (ga0, ga1, ga2, ga3)
    gb = (gb0, gb1, gb2, gb3)
    gc = (gc0, gc1, gc2, gc3)
    gd = (gd0, gd1, gd2, gd3)
    ge = (ge0, ge1, ge2, ge3)

    def index(zz, xx, cc):
        return (zz * X + xx) * C + cc

    def zat(step):
        return lax.rem(z + step + Z, Z)

    peers_z = [{"dp": index(zat(d), x, c), "tensor": tensor} for d in range(1, Z)]
    peer_x = {"dp": index(z, 1 - x, c), "tensor": tensor}
    peer_c = {"dp": index(z, x, 1 - c), "tensor": tensor}
    peer_y = {"dp": dp, "tensor": 1 - tensor}

    started = []

    def send(src, dst, device):
        k = len(started)
        copy = pltpu.make_async_remote_copy(
            src_ref=src,
            dst_ref=dst,
            send_sem=send_sem.at[k],
            recv_sem=recv_sem.at[k],
            device_id=device,
            device_id_type=pl.DeviceIdType.MESH,
        )
        copy.start()
        started.append(copy)
        return copy

    yrecv[:, SENT:ROWS, :] = jnp.zeros((4, ROWS - SENT, yrecv.shape[2]), BF16)
    for j in range(3):
        w0[z, x, c, :, j * TILE : (j + 1) * TILE] = mix_ref[j]
    w1[z, x, c] = outw_ref[...]
    w2[z, x, c] = up_ref[...]
    w3[z, x, c] = down_ref[...]

    barrier = pltpu.get_barrier_semaphore()
    everyone = peers_z + [peer_x, peer_c, peer_y]
    for device in everyone:
        pl.semaphore_signal(barrier, inc=1, device_id=device, device_id_type=pl.DeviceIdType.MESH)
    pl.semaphore_wait(barrier, len(everyone))

    by_z, by_x, by_c, by_d = {}, {}, {}, {}
    for i in range(4):
        mine = w[i].at[z, x, c]
        by_x[i, 0] = send(mine, mine, peer_x)
        for d in range(1, Z):
            by_z[i, d] = send(mine, mine, peers_z[d - 1])
        by_c[i, 0] = send(mine, mine, peer_c)

    def pass_on(i):
        for d in range(1, Z):
            by_z[i, d].wait_recv()
            block = w[i].at[zat(-d), x, c]
            by_x[i, d] = send(block, block, peer_x)
            by_c[i, d] = send(block, block, peer_c)

    def pass_core(i):
        for d in range(Z):
            by_x[i, d].wait_recv()
            block = w[i].at[zat(-d), 1 - x, c]
            by_d[i, d] = send(block, block, peer_c)

    def gathered(i):
        for d in range(Z):
            by_c[i, d].wait_recv()
        for d in range(Z):
            by_d[i, d].wait_recv()

    def weight(i, tile):
        return w[i][:, :, :, :, cols(tile)].reshape(-1, TILE)

    def exchange(k):
        return send(ysend.at[k, pl.ds(0, SENT)], yrecv.at[k, pl.ds(0, SENT)], peer_y)

    def exchanged(k):
        return ysend[k].astype(F32) + yrecv[k].astype(F32)

    def transposed(value):
        return value.astype(F32).T.astype(BF16)

    source = x_ref[...].astype(F32)
    n1, r1, affine = norm_forward(source, fg_ref[...], fs_ref[...])
    n1_s[...] = n1
    a1 = affine.astype(BF16)
    left_t[0] = transposed(a1)
    left_t[1] = transposed(ct_ref[...])
    vs[...] = jnp.zeros_like(vs)
    vs[6:7, :] = jnp.sum(ct_ref[...].astype(F32), axis=0, keepdims=True)
    pass_on(0)
    pass_core(0)
    pass_on(1)
    gathered(0)

    for j in range(3):
        value = jnp.dot(a1, weight(0, j), preferred_element_type=F32)
        if j != 1:
            value = value + ab_ref[j // 2 : j // 2 + 1, :]
        qkv[:, j * TILE : (j + 1) * TILE] = value.astype(BF16)
    pass_core(1)

    heads = TILE // HD
    seen = lax.broadcasted_iota(jnp.int32, (ROWS, ROWS), 1) < SEQ

    def head(ref, part, h):
        pair = ref[:, part * TILE + (h // 2) * 128 : part * TILE + (h // 2) * 128 + 128]
        return pair[:, (h % 2) * HD : (h % 2) * HD + HD]

    halves = []
    for h in range(heads):
        q, k, v = head(qkv, 0, h), head(qkv, 1, h), head(qkv, 2, h)
        scores = jnp.where(seen, nt(q, k) * SCALE, -1e30)
        top = jnp.max(scores, axis=-1, keepdims=True)
        logsum = top + jnp.log(jnp.sum(jnp.exp(scores - top), axis=-1, keepdims=True))
        probs = jnp.exp(scores - logsum)
        prob_s[h] = probs
        halves.append(jnp.dot(probs.astype(BF16), v, preferred_element_type=F32))
        if h % 2 == 1:
            att[:, (h // 2) * 128 : (h // 2) * 128 + 128] = jnp.concatenate(
                halves[-2:], axis=1
            ).astype(BF16)
        if h == 1:
            pass_on(2)
    gathered(1)
    ysend[0] = nt(att[...], weight(1, 0)).astype(BF16)
    first = exchange(0)
    pass_core(2)
    pass_on(3)
    first.wait_recv()
    residual = source + exchanged(0) + ob_ref[...]
    res_s[...] = residual
    n2, r2, affine = norm_forward(residual, sg_ref[...], ss_ref[...])
    n2_s[...] = n2
    a2_s[...] = affine.astype(BF16)
    left_t[2] = transposed(affine.astype(BF16))
    gathered(2)
    tiles = hb_ref.shape[1] // TILE

    def hidden(tile, carry):
        value = jnp.dot(a2_s[...], weight(2, tile), preferred_element_type=F32)
        value, steep = gelu_pair(value + hb_ref[:, cols(tile)])
        active[:, cols(tile)] = value.astype(BF16)
        slope[:, cols(tile)] = steep
        return carry

    lax.fori_loop(0, tiles, hidden, 0)
    pass_core(3)
    gathered(3)

    acc[...] = jnp.zeros_like(acc)

    def second(tile, carry):
        acc[...] += nt(active[:, cols(tile)], weight(3, tile))
        return carry

    lax.fori_loop(0, tiles, second, 0)
    ysend[1] = acc[...].astype(BF16)
    out_copy = exchange(1)

    acc[...] = jnp.zeros_like(acc)

    def back(tile, carry):
        grad = jnp.dot(ct_ref[...], weight(3, tile), preferred_element_type=F32)
        grad = grad * slope[:, cols(tile)]
        sums = jnp.sum(grad, axis=0, keepdims=True)
        slope[0:8, cols(tile)] = jnp.broadcast_to(sums, (8, TILE))
        half = grad.astype(BF16)
        pre_half[:, cols(tile)] = half
        acc[...] += nt(half, weight(2, tile))
        return carry

    lax.fori_loop(0, tiles, back, 0)
    ysend[2] = acc[...].astype(BF16)
    a2_copy = exchange(2)
    vs[4:5, :] = slope[0:1, 0:768]
    vs[5:6, :] = slope[0:1, 768:1536]

    by_a, by_b, by_e = {}, {}, {}

    def gradient(i, left, right, count):
        def one(tile, carry):
            value = jnp.dot(left_t[left], right[:, cols(tile)], preferred_element_type=F32)
            g[i][:, :, :, :, cols(tile)] = value.astype(BF16).reshape(Z, X, C, -1, TILE)
            return carry

        lax.fori_loop(0, count, one, 0)
        by_a[i] = send(g[i].at[:, :, 1 - c], ga[i], peer_c)

    def sum_core(i):
        by_a[i].wait_recv()
        gb[i][...] = (g[i][:, :, c].astype(F32) + ga[i][...].astype(F32)).astype(BF16)
        by_b[i] = send(gb[i].at[:, 1 - x], gc[i], peer_x)

    def sum_x(i):
        by_b[i].wait_recv()
        gd[i][...] = (gb[i][:, x].astype(F32) + gc[i][...].astype(F32)).astype(BF16)
        for d in range(1, Z):
            by_e[i, d] = send(gd[i].at[zat(d)], ge[i].at[d], peers_z[d - 1])

    def sum_z(i):
        total = gd[i][z].astype(F32)
        for d in range(1, Z):
            by_e[i, d].wait_recv()
            total = total + ge[i][d].astype(F32)
        return total

    gradient(3, 1, active, tiles)
    gradient(2, 2, pre_half, tiles)
    sum_core(3)
    out_copy.wait_recv()
    lo_ref[...] = (res_s[...] + exchanged(1) + fb_ref[...]).astype(BF16)
    a2_copy.wait_recv()
    a2_grad = exchanged(2)
    vs[7:8, :] = jnp.sum(a2_grad * n2_s[...], axis=0, keepdims=True)
    vs[8:9, :] = jnp.sum(a2_grad, axis=0, keepdims=True)
    res_grad = ct_ref[...].astype(F32) + norm_backward(a2_grad, n2_s[...], r2, sg_ref[...])
    rg_s[...] = res_grad
    vs[3:4, :] = jnp.sum(res_grad, axis=0, keepdims=True)
    res_half = res_grad.astype(BF16)
    left_t[1] = transposed(res_half)
    sum_core(2)
    attg[...] = jnp.dot(res_half, weight(1, 0), preferred_element_type=F32).astype(BF16)
    gradient(1, 1, att, 1)
    sum_x(3)

    pairs = {}
    for h in range(heads):
        q, k, v = head(qkv, 0, h), head(qkv, 1, h), head(qkv, 2, h)
        upper = head(attg, 0, h)
        probs = prob_s[h]
        prob_grad = nt(upper, v)
        delta = jnp.sum(probs * prob_grad, axis=-1, keepdims=True)
        score_grad = (probs * (prob_grad - delta) * SCALE).astype(BF16)
        pairs[0, h] = jnp.dot(score_grad, k, preferred_element_type=F32)
        pairs[1, h] = tn(score_grad, q)
        pairs[2, h] = tn(probs.astype(BF16), upper)
        if h % 2 == 1:
            start = (h // 2) * 128
            for j in range(3):
                pair = jnp.concatenate([pairs[j, h - 1], pairs[j, h]], axis=1)
                stacked[:, j * TILE + start : j * TILE + start + 128] = pair.astype(BF16)
                if j != 1:
                    place = (j // 2) * TILE + start
                    vs[2:3, place : place + 128] = jnp.sum(pair, axis=0, keepdims=True)
        if h == 1:
            sum_core(1)
        if h == 3:
            sum_x(2)
    total = nt(stacked[:, 0:TILE], weight(0, 0))
    for j in range(1, 3):
        total = total + nt(stacked[:, j * TILE : (j + 1) * TILE], weight(0, j))
    ysend[3] = total.astype(BF16)
    last = exchange(3)
    gradient(0, 0, stacked, 3)
    sum_x(1)
    last.wait_recv()
    a1_grad = exchanged(3)
    vs[0:1, :] = jnp.sum(a1_grad * n1_s[...], axis=0, keepdims=True)
    vs[1:2, :] = jnp.sum(a1_grad, axis=0, keepdims=True)
    vec_c = send(vs, vr.at[0], peer_c)
    sum_core(0)
    ig_ref[...] = (rg_s[...] + norm_backward(a1_grad, n1_s[...], r1, fg_ref[...])).astype(BF16)
    vec_c.wait_recv()
    vr[1] = vs[...] + vr[0]
    vec_x = send(vr.at[1], vr.at[2], peer_x)
    gdown_ref[...] = sum_z(3)
    gup_ref[...] = sum_z(2)
    vec_x.wait_recv()
    mine = vr[1] + vr[2]
    vr[3 + z] = mine
    vec_z = [send(vr.at[3 + z], vr.at[3 + z], peers_z[d - 1]) for d in range(1, Z)]
    sum_x(0)
    gout_ref[...] = sum_z(1)
    for copy in vec_z:
        copy.wait_recv()
    total = vr[3]
    for d in range(1, Z):
        total = total + vr[3 + d]
    vec_ref[...] = total
    total = sum_z(0)
    for j in range(3):
        gmix_ref[j] = total[:, j * TILE : (j + 1) * TILE]
    for copy in started:
        copy.wait_send()
    assert len(started) == copies


def local(sizes, *arrays):
    n = sizes["dp"]
    inputs, mixing, up = arrays[0], arrays[2], arrays[4]
    shard = mixing.shape[1]
    fits = (
        shard % 16 == 0
        and n % (X * C) == 0
        and sizes["tensor"] == 2
        and inputs.shape == (SEQ, 768)
        and mixing.shape[2] == TILE
        and up.shape[1] == 1536
    )
    if not fits:
        return local_plain(*arrays)
    (
        inputs,
        cotangent,
        mixing,
        output,
        up,
        down,
        first_gain,
        first_shift,
        attend_bias,
        output_bias,
        hidden_bias,
        final_bias,
        second_gain,
        second_shift,
    ) = arrays
    Z = n // (X * C)
    width = inputs.shape[1]
    sizes_of = (3 * TILE, TILE, up.shape[1], up.shape[1])
    pad = ((0, ROWS - SEQ), (0, 0))
    copies = 4 * (Z - 1 + 3 * Z) + 4 + 4 * (Z + 1) + Z + 1
    vmem = pl.BlockSpec(memory_space=pltpu.VMEM)
    full = [pltpu.VMEM((Z, X, C, shard, k), BF16) for k in sizes_of]
    half = [pltpu.VMEM((Z, X, shard, k), BF16) for k in sizes_of]
    quarter = [pltpu.VMEM((Z, shard, k), BF16) for k in sizes_of]
    outs = pl.pallas_call(
        functools.partial(layer_kernel, Z, copies),
        out_shape=(
            jax.ShapeDtypeStruct((ROWS, width), BF16),
            jax.ShapeDtypeStruct((ROWS, width), BF16),
            jax.ShapeDtypeStruct((3, shard, TILE), F32),
            jax.ShapeDtypeStruct((shard, TILE), F32),
            jax.ShapeDtypeStruct((shard, up.shape[1]), F32),
            jax.ShapeDtypeStruct((shard, up.shape[1]), F32),
            jax.ShapeDtypeStruct((16, width), F32),
        ),
        in_specs=[vmem] * 14,
        out_specs=(vmem,) * 7,
        scratch_shapes=full
        + full
        + half
        + half
        + quarter
        + quarter
        + quarter
        + [
            pltpu.VMEM((4, ROWS, width), BF16),
            pltpu.VMEM((4, ROWS, width), BF16),
            pltpu.VMEM((16, width), F32),
            pltpu.VMEM((3 + Z, 16, width), F32),
            pltpu.VMEM((3, width, ROWS), BF16),
            pltpu.VMEM((ROWS, width), F32),
            pltpu.VMEM((ROWS, width), F32),
            pltpu.VMEM((ROWS, width), F32),
            pltpu.VMEM((ROWS, 3 * TILE), BF16),
            pltpu.VMEM((TILE // HD, ROWS, ROWS), F32),
            pltpu.VMEM((ROWS, TILE), BF16),
            pltpu.VMEM((ROWS, TILE), BF16),
            pltpu.VMEM((ROWS, 3 * TILE), BF16),
            pltpu.VMEM((ROWS, up.shape[1]), BF16),
            pltpu.VMEM((ROWS, up.shape[1]), F32),
            pltpu.VMEM((ROWS, up.shape[1]), BF16),
            pltpu.VMEM((ROWS, width), BF16),
            pltpu.VMEM((ROWS, width), F32),
            pltpu.VMEM((ROWS, width), F32),
            pltpu.SemaphoreType.DMA((copies,)),
            pltpu.SemaphoreType.DMA((copies,)),
        ],
        compiler_params=pltpu.CompilerParams(
            collective_id=0, has_side_effects=True, vmem_limit_bytes=60 * 1024 * 1024
        ),
    )(
        jnp.pad(inputs, pad),
        jnp.pad(cotangent, pad),
        mixing,
        output.T,
        up,
        down.T,
        first_gain.reshape(1, -1),
        first_shift.reshape(1, -1),
        attend_bias,
        output_bias.reshape(1, -1),
        hidden_bias.reshape(1, -1),
        final_bias.reshape(1, -1),
        second_gain.reshape(1, -1),
        second_shift.reshape(1, -1),
    )
    layer_output, input_grad, gmix, gout, gup, gdown, vec = outs
    return (
        layer_output[:SEQ],
        input_grad[:SEQ],
        gmix,
        gout.T,
        gup,
        gdown.T,
        vec[0],
        vec[1],
        vec[2].reshape(2, TILE),
        vec[3],
        vec[4:6].reshape(-1),
        vec[6],
        vec[7],
        vec[8],
    )


def solution(mesh):
    placed = (
        P("dp", None),
        P("dp", None),
        P(None, "dp", "tensor"),
        P("tensor", "dp"),
        P("dp", "tensor"),
        P("tensor", "dp"),
        P(),
        P(),
        P(None, "tensor"),
        P(),
        P("tensor"),
        P(),
        P(),
        P(),
    )
    return jax.shard_map(
        functools.partial(local, dict(mesh.shape)),
        mesh=mesh,
        in_specs=placed,
        out_specs=(
            P("dp", None),
            P("dp", None),
            P(None, "dp", "tensor"),
            P("tensor", "dp"),
            P("dp", "tensor"),
            P("tensor", "dp"),
            P(),
            P(),
            P(None, "tensor"),
            P(),
            P("tensor"),
            P(),
            P(),
            P(),
        ),
        check_vma=False,
    )
```

```python
import functools

import jax
import jax.numpy as jnp
from jax import lax
from jax.experimental import pallas as pl
from jax.experimental.pallas import tpu as pltpu
from jax.sharding import PartitionSpec as P

HD = 64
SEQ = 197


EPSILON = 1e-06


def norm_forward(values, gain, shift):
    center = values - jnp.mean(values, axis=-1, keepdims=True)
    inverse = lax.rsqrt(jnp.mean(center * center, axis=-1, keepdims=True) + EPSILON)
    normed = center * inverse
    return (normed, inverse, normed * gain + shift)


def norm_backward(upstream, normed, inverse, gain):
    scaled = upstream * gain
    return inverse * (
        scaled
        - jnp.mean(scaled, axis=-1, keepdims=True)
        - normed * jnp.mean(scaled * normed, axis=-1, keepdims=True)
    )


def gelu_pair(values):
    normal_cdf = 0.5 * (1.0 + lax.erf(values * 0.7071067811865476))
    density = 0.3989422804014327 * jnp.exp(-0.5 * values * values)
    return (values * normal_cdf, normal_cdf + values * density)


def matmul(left, right):
    return jnp.dot(left, right, preferred_element_type=jnp.float32)


def local_plain(
    inputs,
    cotangent,
    mixing_weight,
    output_weight,
    up_weight,
    down_weight,
    first_gain,
    first_shift,
    attend_bias,
    output_bias,
    hidden_bias,
    final_bias,
    second_gain,
    second_shift,
):
    mixing_full, output_full, up_full, down_full = (
        lax.all_gather(mixing_weight, "dp", axis=1, tiled=True),
        lax.all_gather(output_weight, "dp", axis=1, tiled=True),
        lax.all_gather(up_weight, "dp", axis=0, tiled=True),
        lax.all_gather(down_weight, "dp", axis=1, tiled=True),
    )
    row_count = inputs.shape[0]
    images = row_count // SEQ
    width = mixing_full.shape[2]
    split_shape = (images, SEQ, width // HD, HD)
    scale = HD ** (-0.5)
    source = inputs.astype(jnp.float32)
    normed_one, inverse_one, affine_one = norm_forward(source, first_gain, first_shift)
    mixed_in = affine_one.astype(jnp.bfloat16)
    projected = jnp.einsum("nd,jde->jne", mixed_in, mixing_full, preferred_element_type=jnp.float32)
    query = (projected[0] + attend_bias[0]).astype(jnp.bfloat16).reshape(split_shape)
    keys = projected[1].astype(jnp.bfloat16).reshape(split_shape)
    values = (projected[2] + attend_bias[1]).astype(jnp.bfloat16).reshape(split_shape)
    scores = jnp.einsum("bqhd,bkhd->bhqk", query, keys, preferred_element_type=jnp.float32) * scale
    top = jnp.max(scores, axis=-1, keepdims=True)
    logsum = top + jnp.log(jnp.sum(jnp.exp(scores - top), axis=-1, keepdims=True))
    probs = jnp.exp(scores - logsum).astype(jnp.bfloat16)
    attended = (
        jnp.einsum("bhqk,bkhd->bqhd", probs, values, preferred_element_type=jnp.float32)
        .astype(jnp.bfloat16)
        .reshape(row_count, width)
    )
    residual = source + lax.psum(matmul(attended, output_full), "tensor") + output_bias
    normed_two, inverse_two, affine_two = norm_forward(residual, second_gain, second_shift)
    hidden_in = affine_two.astype(jnp.bfloat16)
    preact = matmul(hidden_in, up_full) + hidden_bias
    active_full, slope = gelu_pair(preact)
    active = active_full.astype(jnp.bfloat16)
    layer_output = (residual + lax.psum(matmul(active, down_full), "tensor") + final_bias).astype(
        jnp.bfloat16
    )
    mixing_back, output_back, up_back, down_back = (mixing_full, output_full, up_full, down_full)
    upstream = cotangent.astype(jnp.float32)
    down_grad = matmul(active.T, cotangent)
    finalbias_grad = jnp.sum(upstream, axis=0)
    pre_grad = matmul(cotangent, down_back.T) * slope
    pre_half = pre_grad.astype(jnp.bfloat16)
    up_grad = matmul(hidden_in.T, pre_half)
    hiddenbias_grad = jnp.sum(pre_grad, axis=0)
    affine_two_grad = lax.psum(matmul(pre_half, up_back.T), "tensor")
    secondgain_grad = jnp.sum(affine_two_grad * normed_two, axis=0)
    secondshift_grad = jnp.sum(affine_two_grad, axis=0)
    residual_grad = upstream + norm_backward(affine_two_grad, normed_two, inverse_two, second_gain)
    residual_half = residual_grad.astype(jnp.bfloat16)
    outweight_grad = matmul(attended.T, residual_half)
    outbias_grad = jnp.sum(residual_grad, axis=0)
    attended_grad = matmul(residual_half, output_back.T).astype(jnp.bfloat16).reshape(split_shape)
    recomputed = (
        jnp.einsum("bqhd,bkhd->bhqk", query, keys, preferred_element_type=jnp.float32) * scale
    )
    probs_full = jnp.exp(recomputed - logsum)
    prob_grad = jnp.einsum(
        "bqhd,bkhd->bhqk", attended_grad, values, preferred_element_type=jnp.float32
    )
    delta = jnp.sum(probs_full * prob_grad, axis=-1, keepdims=True)
    score_grad = (probs_full * (prob_grad - delta) * scale).astype(jnp.bfloat16)
    query_grad = jnp.einsum(
        "bhqk,bkhd->bqhd", score_grad, keys, preferred_element_type=jnp.float32
    ).reshape(row_count, width)
    keys_grad = jnp.einsum(
        "bhqk,bqhd->bkhd", score_grad, query, preferred_element_type=jnp.float32
    ).reshape(row_count, width)
    values_grad = jnp.einsum(
        "bhqk,bqhd->bkhd", probs, attended_grad, preferred_element_type=jnp.float32
    ).reshape(row_count, width)
    attendbias_grad = jnp.stack([jnp.sum(query_grad, axis=0), jnp.sum(values_grad, axis=0)])
    stacked = jnp.stack([query_grad, keys_grad, values_grad]).astype(jnp.bfloat16)
    mixing_grad = jnp.einsum("nd,jne->jde", mixed_in, stacked, preferred_element_type=jnp.float32)
    affine_one_grad = lax.psum(
        jnp.einsum("jne,jde->nd", stacked, mixing_back, preferred_element_type=jnp.float32),
        "tensor",
    )
    firstgain_grad = jnp.sum(affine_one_grad * normed_one, axis=0)
    firstshift_grad = jnp.sum(affine_one_grad, axis=0)
    input_grad = (
        residual_grad + norm_backward(affine_one_grad, normed_one, inverse_one, first_gain)
    ).astype(jnp.bfloat16)
    mixing_share, output_share, up_share, down_share = (
        lax.psum_scatter(mixing_grad, "dp", scatter_dimension=1, tiled=True),
        lax.psum_scatter(outweight_grad, "dp", scatter_dimension=1, tiled=True),
        lax.psum_scatter(up_grad, "dp", scatter_dimension=0, tiled=True),
        lax.psum_scatter(down_grad, "dp", scatter_dimension=1, tiled=True),
    )
    vector_totals = lax.psum(
        (
            firstgain_grad,
            firstshift_grad,
            attendbias_grad,
            outbias_grad,
            hiddenbias_grad,
            finalbias_grad,
            secondgain_grad,
            secondshift_grad,
        ),
        "dp",
    )
    return (
        layer_output,
        input_grad,
        mixing_share,
        output_share,
        up_share,
        down_share,
        vector_totals[0],
        vector_totals[1],
        vector_totals[2],
        vector_totals[3],
        vector_totals[4],
        vector_totals[5],
        vector_totals[6],
        vector_totals[7],
    )


ROWS = 256
SENT = 208
X = 2
C = 2
TILE = 384
SCALE = HD ** (-0.5)
F32 = jnp.float32
BF16 = jnp.bfloat16


def nt(left, right):
    return lax.dot_general(left, right, (((1,), (1,)), ((), ())), preferred_element_type=F32)


def tn(left, right):
    return lax.dot_general(left, right, (((0,), (0,)), ((), ())), preferred_element_type=F32)


def cols(tile):
    return pl.ds(pl.multiple_of(tile * TILE, TILE), TILE)


def layer_kernel(
    Z,
    copies,
    x_ref,
    ct_ref,
    mix_ref,
    outw_ref,
    up_ref,
    down_ref,
    fg_ref,
    fs_ref,
    ab_ref,
    ob_ref,
    hb_ref,
    fb_ref,
    sg_ref,
    ss_ref,
    lo_ref,
    ig_ref,
    gmix_ref,
    gout_ref,
    gup_ref,
    gdown_ref,
    vec_ref,
    w0,
    w1,
    w2,
    w3,
    g0,
    g1,
    g2,
    g3,
    ga0,
    ga1,
    ga2,
    ga3,
    gb0,
    gb1,
    gb2,
    gb3,
    gc0,
    gc1,
    gc2,
    gc3,
    gd0,
    gd1,
    gd2,
    gd3,
    ge0,
    ge1,
    ge2,
    ge3,
    ysend,
    yrecv,
    vs,
    vr,
    left_t,
    n1_s,
    n2_s,
    acc,
    qkv,
    prob_s,
    att,
    attg,
    stacked,
    active,
    slope,
    pre_half,
    a2_s,
    res_s,
    rg_s,
    ct_s,
    rows_s,
    send_sem,
    recv_sem,
):
    dp = lax.axis_index("dp")
    tensor = lax.axis_index("tensor")
    c = lax.rem(dp, C)
    x = lax.rem(dp // C, X)
    z = dp // (C * X)
    w = (w0, w1, w2, w3)
    g = (g0, g1, g2, g3)
    ga = (ga0, ga1, ga2, ga3)
    gb = (gb0, gb1, gb2, gb3)
    gc = (gc0, gc1, gc2, gc3)
    gd = (gd0, gd1, gd2, gd3)
    ge = (ge0, ge1, ge2, ge3)

    def index(zz, xx, cc):
        return (zz * X + xx) * C + cc

    def zat(step):
        return lax.rem(z + step + Z, Z)

    peers_z = [{"dp": index(zat(d), x, c), "tensor": tensor} for d in range(1, Z)]
    peer_x = {"dp": index(z, 1 - x, c), "tensor": tensor}
    peer_c = {"dp": index(z, x, 1 - c), "tensor": tensor}
    peer_y = {"dp": dp, "tensor": 1 - tensor}

    started = []

    def send(src, dst, device):
        k = len(started)
        copy = pltpu.make_async_remote_copy(
            src_ref=src,
            dst_ref=dst,
            send_sem=send_sem.at[k],
            recv_sem=recv_sem.at[k],
            device_id=device,
            device_id_type=pl.DeviceIdType.MESH,
        )
        copy.start()
        started.append(copy)
        return copy

    yrecv[:, SENT:ROWS, :] = jnp.zeros((4, ROWS - SENT, yrecv.shape[2]), BF16)
    for j in range(3):
        w0[z, x, c, :, j * TILE : (j + 1) * TILE] = mix_ref[j]
    w1[z, x, c] = outw_ref[...]
    w2[z, x, c] = up_ref[...]
    w3[z, x, c] = down_ref[...]

    barrier = pltpu.get_barrier_semaphore()
    everyone = peers_z + [peer_x, peer_c, peer_y]
    for device in everyone:
        pl.semaphore_signal(barrier, inc=1, device_id=device, device_id_type=pl.DeviceIdType.MESH)
    pl.semaphore_wait(barrier, len(everyone))

    by_z, by_x, by_c, by_d = {}, {}, {}, {}

    def own(i):
        mine = w[i].at[z, x, c]
        by_x[i, 0] = send(mine, mine, peer_x)
        for d in range(1, Z):
            by_z[i, d] = send(mine, mine, peers_z[d - 1])
        by_c[i, 0] = send(mine, mine, peer_c)

    own(0)
    own(1)

    def pass_on(i):
        for d in range(1, Z):
            by_z[i, d].wait_recv()
            block = w[i].at[zat(-d), x, c]
            by_x[i, d] = send(block, block, peer_x)
            by_c[i, d] = send(block, block, peer_c)

    def pass_core(i):
        for d in range(Z):
            by_x[i, d].wait_recv()
            block = w[i].at[zat(-d), 1 - x, c]
            by_d[i, d] = send(block, block, peer_c)

    def gathered(i):
        for d in range(Z):
            by_c[i, d].wait_recv()
        for d in range(Z):
            by_d[i, d].wait_recv()

    def weight(i, tile):
        return w[i][:, :, :, :, cols(tile)].reshape(-1, TILE)

    def exchange(k):
        return send(ysend.at[k, pl.ds(0, SENT)], yrecv.at[k, pl.ds(0, SENT)], peer_y)

    def exchanged(k):
        return ysend[k].astype(F32) + yrecv[k].astype(F32)

    def transposed(value):
        return value.astype(F32).T.astype(BF16)

    rg_s[192:ROWS, :] = jnp.zeros((ROWS - 192, rg_s.shape[1]), F32)
    rg_s[0:SEQ, :] = x_ref[...].astype(F32)
    acc[192:ROWS, :] = jnp.zeros((ROWS - 192, acc.shape[1]), F32)
    acc[0:SEQ, :] = ct_ref[...].astype(F32)
    ct_s[...] = acc[...].astype(BF16)
    for row, ref in enumerate((fg_ref, fs_ref, ob_ref, fb_ref, sg_ref)):
        rows_s[row : row + 1, 0:768] = ref[...].reshape(1, -1)
    rows_s[0:1, 768:1536] = ss_ref[...].reshape(1, -1)
    rows_s[5:6, :] = hb_ref[...].reshape(1, -1)
    fg_row, fs_row, ob_row, fb_row, sg_row = (rows_s.at[r : r + 1, 0:768] for r in range(5))
    ss_row = rows_s.at[0:1, 768:1536]
    source = rg_s[...]
    n1, r1, affine = norm_forward(source, fg_row[...], fs_row[...])
    n1_s[...] = n1
    a1 = affine.astype(BF16)
    left_t[0] = transposed(a1)
    left_t[1] = transposed(ct_s[...])
    vs[...] = jnp.zeros_like(vs)
    vs[6:7, :] = jnp.sum(ct_s[...].astype(F32), axis=0, keepdims=True)
    pass_on(0)
    own(2)
    pass_core(0)
    pass_on(1)
    own(3)
    gathered(0)

    for j in range(3):
        value = jnp.dot(a1, weight(0, j), preferred_element_type=F32)
        if j != 1:
            value = value + ab_ref[j // 2 : j // 2 + 1, :]
        qkv[:, j * TILE : (j + 1) * TILE] = value.astype(BF16)
    pass_core(1)

    heads = TILE // HD
    seen = lax.broadcasted_iota(jnp.int32, (ROWS, ROWS), 1) < SEQ

    def head(ref, part, h):
        pair = ref[:, part * TILE + (h // 2) * 128 : part * TILE + (h // 2) * 128 + 128]
        return pair[:, (h % 2) * HD : (h % 2) * HD + HD]

    halves = []
    for h in range(heads):
        q, k, v = head(qkv, 0, h), head(qkv, 1, h), head(qkv, 2, h)
        scores = jnp.where(seen, nt(q, k) * SCALE, -1e30)
        top = jnp.max(scores, axis=-1, keepdims=True)
        logsum = top + jnp.log(jnp.sum(jnp.exp(scores - top), axis=-1, keepdims=True))
        probs = jnp.exp(scores - logsum)
        prob_s[h] = probs
        halves.append(jnp.dot(probs.astype(BF16), v, preferred_element_type=F32))
        if h % 2 == 1:
            att[:, (h // 2) * 128 : (h // 2) * 128 + 128] = jnp.concatenate(
                halves[-2:], axis=1
            ).astype(BF16)
        if h == 1:
            pass_on(2)
    gathered(1)
    ysend[0] = nt(att[...], weight(1, 0)).astype(BF16)
    first = exchange(0)
    pass_core(2)
    pass_on(3)
    first.wait_recv()
    residual = source + exchanged(0) + ob_row[...]
    res_s[...] = residual
    n2, r2, affine = norm_forward(residual, sg_row[...], ss_row[...])
    n2_s[...] = n2
    a2_s[...] = affine.astype(BF16)
    left_t[2] = transposed(affine.astype(BF16))
    gathered(2)
    tiles = hb_ref.shape[0] // TILE

    def hidden(tile, carry):
        value = jnp.dot(a2_s[...], weight(2, tile), preferred_element_type=F32)
        value, steep = gelu_pair(value + rows_s[5:6, cols(tile)])
        active[:, cols(tile)] = value.astype(BF16)
        slope[:, cols(tile)] = steep
        return carry

    lax.fori_loop(0, tiles, hidden, 0)
    pass_core(3)
    by_a, by_b, by_e = {}, {}, {}

    def gradient(i, left, right, count):
        def one(tile, carry):
            value = jnp.dot(left_t[left], right[:, cols(tile)], preferred_element_type=F32)
            g[i][:, :, :, :, cols(tile)] = value.astype(BF16).reshape(Z, X, C, -1, TILE)
            return carry

        lax.fori_loop(0, count, one, 0)
        by_a[i] = send(g[i].at[:, :, 1 - c], ga[i], peer_c)

    def sum_core(i):
        by_a[i].wait_recv()
        gb[i][...] = (g[i][:, :, c].astype(F32) + ga[i][...].astype(F32)).astype(BF16)
        by_b[i] = send(gb[i].at[:, 1 - x], gc[i], peer_x)

    def sum_x(i):
        by_b[i].wait_recv()
        gd[i][...] = (gb[i][:, x].astype(F32) + gc[i][...].astype(F32)).astype(BF16)
        for d in range(1, Z):
            by_e[i, d] = send(gd[i].at[zat(d)], ge[i].at[d], peers_z[d - 1])

    def sum_z(i):
        total = gd[i][z].astype(F32)
        for d in range(1, Z):
            by_e[i, d].wait_recv()
            total = total + ge[i][d].astype(F32)
        return total

    gradient(3, 1, active, tiles)
    gathered(3)

    acc[...] = jnp.zeros_like(acc)

    def second(tile, carry):
        acc[...] += nt(active[:, cols(tile)], weight(3, tile))
        return carry

    lax.fori_loop(0, tiles, second, 0)
    ysend[1] = acc[...].astype(BF16)
    out_copy = exchange(1)
    sum_core(3)

    acc[...] = jnp.zeros_like(acc)

    def back(tile, carry):
        grad = jnp.dot(ct_s[...], weight(3, tile), preferred_element_type=F32)
        grad = grad * slope[:, cols(tile)]
        sums = jnp.sum(grad, axis=0, keepdims=True)
        slope[0:8, cols(tile)] = jnp.broadcast_to(sums, (8, TILE))
        half = grad.astype(BF16)
        pre_half[:, cols(tile)] = half
        acc[...] += nt(half, weight(2, tile))
        return carry

    lax.fori_loop(0, tiles, back, 0)
    ysend[2] = acc[...].astype(BF16)
    a2_copy = exchange(2)
    vs[4:5, :] = slope[0:1, 0:768]
    vs[5:6, :] = slope[0:1, 768:1536]

    gradient(2, 2, pre_half, tiles)
    out_copy.wait_recv()
    lo_ref[...] = (res_s[...] + exchanged(1) + fb_row[...]).astype(BF16)
    a2_copy.wait_recv()
    a2_grad = exchanged(2)
    vs[7:8, :] = jnp.sum(a2_grad * n2_s[...], axis=0, keepdims=True)
    vs[8:9, :] = jnp.sum(a2_grad, axis=0, keepdims=True)
    res_grad = ct_s[...].astype(F32) + norm_backward(a2_grad, n2_s[...], r2, sg_row[...])
    rg_s[...] = res_grad
    vs[3:4, :] = jnp.sum(res_grad, axis=0, keepdims=True)
    res_half = res_grad.astype(BF16)
    left_t[1] = transposed(res_half)
    sum_core(2)
    sum_x(3)
    attg[...] = jnp.dot(res_half, weight(1, 0), preferred_element_type=F32).astype(BF16)
    gradient(1, 1, att, 1)

    pairs = {}
    for h in range(heads):
        q, k, v = head(qkv, 0, h), head(qkv, 1, h), head(qkv, 2, h)
        upper = head(attg, 0, h)
        probs = prob_s[h]
        prob_grad = nt(upper, v)
        delta = jnp.sum(probs * prob_grad, axis=-1, keepdims=True)
        score_grad = (probs * (prob_grad - delta) * SCALE).astype(BF16)
        pairs[0, h] = jnp.dot(score_grad, k, preferred_element_type=F32)
        pairs[1, h] = tn(score_grad, q)
        pairs[2, h] = tn(probs.astype(BF16), upper)
        if h % 2 == 1:
            start = (h // 2) * 128
            for j in range(3):
                pair = jnp.concatenate([pairs[j, h - 1], pairs[j, h]], axis=1)
                stacked[:, j * TILE + start : j * TILE + start + 128] = pair.astype(BF16)
                if j != 1:
                    place = (j // 2) * TILE + start
                    vs[2:3, place : place + 128] = jnp.sum(pair, axis=0, keepdims=True)
        if h == 1:
            sum_core(1)
        if h == 3:
            sum_x(2)
    total = nt(stacked[:, 0:TILE], weight(0, 0))
    for j in range(1, 3):
        total = total + nt(stacked[:, j * TILE : (j + 1) * TILE], weight(0, j))
    ysend[3] = total.astype(BF16)
    last = exchange(3)
    gradient(0, 0, stacked, 3)
    sum_x(1)
    last.wait_recv()
    a1_grad = exchanged(3)
    vs[0:1, :] = jnp.sum(a1_grad * n1_s[...], axis=0, keepdims=True)
    vs[1:2, :] = jnp.sum(a1_grad, axis=0, keepdims=True)
    vec_c = send(vs, vr.at[0], peer_c)
    sum_core(0)
    ig_ref[...] = (rg_s[...] + norm_backward(a1_grad, n1_s[...], r1, fg_row[...])).astype(BF16)
    vec_c.wait_recv()
    vr[1] = vs[...] + vr[0]
    vec_x = send(vr.at[1], vr.at[2], peer_x)
    gdown_ref[...] = sum_z(3)
    gup_ref[...] = sum_z(2)
    vec_x.wait_recv()
    mine = vr[1] + vr[2]
    vr[3 + z] = mine
    vec_z = [send(vr.at[3 + z], vr.at[3 + z], peers_z[d - 1]) for d in range(1, Z)]
    sum_x(0)
    gout_ref[...] = sum_z(1)
    for copy in vec_z:
        copy.wait_recv()
    total = vr[3]
    for d in range(1, Z):
        total = total + vr[3 + d]
    vec_ref[...] = total
    total = sum_z(0)
    for j in range(3):
        gmix_ref[j] = total[:, j * TILE : (j + 1) * TILE]
    for copy in started:
        copy.wait_send()
    assert len(started) == copies


def local(sizes, *arrays):
    n = sizes["dp"]
    inputs, mixing, up = arrays[0], arrays[2], arrays[4]
    shard = mixing.shape[1]
    fits = (
        shard % 16 == 0
        and n % (X * C) == 0
        and sizes["tensor"] == 2
        and inputs.shape == (SEQ, 768)
        and mixing.shape[2] == TILE
        and up.shape[1] == 1536
    )
    if not fits:
        return local_plain(*arrays)
    (
        inputs,
        cotangent,
        mixing,
        output,
        up,
        down,
        first_gain,
        first_shift,
        attend_bias,
        output_bias,
        hidden_bias,
        final_bias,
        second_gain,
        second_shift,
    ) = arrays
    Z = n // (X * C)
    width = inputs.shape[1]
    sizes_of = (3 * TILE, TILE, up.shape[1], up.shape[1])
    copies = 4 * (Z - 1 + 3 * Z) + 4 + 4 * (Z + 1) + Z + 1
    vmem = pl.BlockSpec(memory_space=pltpu.VMEM)
    full = [pltpu.VMEM((Z, X, C, shard, k), BF16) for k in sizes_of]
    half = [pltpu.VMEM((Z, X, shard, k), BF16) for k in sizes_of]
    quarter = [pltpu.VMEM((Z, shard, k), BF16) for k in sizes_of]
    outs = pl.pallas_call(
        functools.partial(layer_kernel, Z, copies),
        out_shape=(
            jax.ShapeDtypeStruct((ROWS, width), BF16),
            jax.ShapeDtypeStruct((ROWS, width), BF16),
            jax.ShapeDtypeStruct((3, shard, TILE), F32),
            jax.ShapeDtypeStruct((shard, TILE), F32),
            jax.ShapeDtypeStruct((shard, up.shape[1]), F32),
            jax.ShapeDtypeStruct((shard, up.shape[1]), F32),
            jax.ShapeDtypeStruct((16, width), F32),
        ),
        in_specs=[vmem] * 14,
        out_specs=(vmem,) * 7,
        scratch_shapes=full
        + full
        + half
        + half
        + quarter
        + quarter
        + quarter
        + [
            pltpu.VMEM((4, ROWS, width), BF16),
            pltpu.VMEM((4, ROWS, width), BF16),
            pltpu.VMEM((16, width), F32),
            pltpu.VMEM((3 + Z, 16, width), F32),
            pltpu.VMEM((3, width, ROWS), BF16),
            pltpu.VMEM((ROWS, width), F32),
            pltpu.VMEM((ROWS, width), F32),
            pltpu.VMEM((ROWS, width), F32),
            pltpu.VMEM((ROWS, 3 * TILE), BF16),
            pltpu.VMEM((TILE // HD, ROWS, ROWS), F32),
            pltpu.VMEM((ROWS, TILE), BF16),
            pltpu.VMEM((ROWS, TILE), BF16),
            pltpu.VMEM((ROWS, 3 * TILE), BF16),
            pltpu.VMEM((ROWS, up.shape[1]), BF16),
            pltpu.VMEM((ROWS, up.shape[1]), F32),
            pltpu.VMEM((ROWS, up.shape[1]), BF16),
            pltpu.VMEM((ROWS, width), BF16),
            pltpu.VMEM((ROWS, width), F32),
            pltpu.VMEM((ROWS, width), F32),
            pltpu.VMEM((ROWS, width), BF16),
            pltpu.VMEM((6, up.shape[1]), F32),
            pltpu.SemaphoreType.DMA((copies,)),
            pltpu.SemaphoreType.DMA((copies,)),
        ],
        compiler_params=pltpu.CompilerParams(
            collective_id=0, has_side_effects=True, vmem_limit_bytes=60 * 1024 * 1024
        ),
    )(
        inputs,
        cotangent,
        mixing,
        output.T,
        up,
        down.T,
        first_gain,
        first_shift,
        attend_bias,
        output_bias,
        hidden_bias,
        final_bias,
        second_gain,
        second_shift,
    )
    layer_output, input_grad, gmix, gout, gup, gdown, vec = outs
    return (
        layer_output[:SEQ],
        input_grad[:SEQ],
        gmix,
        gout.T,
        gup,
        gdown.T,
        vec[0],
        vec[1],
        vec[2].reshape(2, TILE),
        vec[3],
        vec[4:6].reshape(-1),
        vec[6],
        vec[7],
        vec[8],
    )


def solution(mesh):
    placed = (
        P("dp", None),
        P("dp", None),
        P(None, "dp", "tensor"),
        P("tensor", "dp"),
        P("dp", "tensor"),
        P("tensor", "dp"),
        P(),
        P(),
        P(None, "tensor"),
        P(),
        P("tensor"),
        P(),
        P(),
        P(),
    )
    return jax.shard_map(
        functools.partial(local, dict(mesh.shape)),
        mesh=mesh,
        in_specs=placed,
        out_specs=(
            P("dp", None),
            P("dp", None),
            P(None, "dp", "tensor"),
            P("tensor", "dp"),
            P("dp", "tensor"),
            P("tensor", "dp"),
            P(),
            P(),
            P(None, "tensor"),
            P(),
            P("tensor"),
            P(),
            P(),
            P(),
        ),
        check_vma=False,
    )
```

```python
import functools

import jax
import jax.numpy as jnp
from jax import lax
from jax.experimental import pallas as pl
from jax.experimental.pallas import tpu as pltpu
from jax.sharding import PartitionSpec as P

HD = 64
SEQ = 197


EPSILON = 1e-06


def norm_forward(values, gain, shift):
    center = values - jnp.mean(values, axis=-1, keepdims=True)
    inverse = lax.rsqrt(jnp.mean(center * center, axis=-1, keepdims=True) + EPSILON)
    normed = center * inverse
    return (normed, inverse, normed * gain + shift)


def norm_backward(upstream, normed, inverse, gain):
    scaled = upstream * gain
    return inverse * (
        scaled
        - jnp.mean(scaled, axis=-1, keepdims=True)
        - normed * jnp.mean(scaled * normed, axis=-1, keepdims=True)
    )


def gelu_pair(values):
    normal_cdf = 0.5 * (1.0 + lax.erf(values * 0.7071067811865476))
    density = 0.3989422804014327 * jnp.exp(-0.5 * values * values)
    return (values * normal_cdf, normal_cdf + values * density)


def matmul(left, right):
    return jnp.dot(left, right, preferred_element_type=jnp.float32)


def local_plain(
    inputs,
    cotangent,
    mixing_weight,
    output_weight,
    up_weight,
    down_weight,
    first_gain,
    first_shift,
    attend_bias,
    output_bias,
    hidden_bias,
    final_bias,
    second_gain,
    second_shift,
):
    mixing_full, output_full, up_full, down_full = (
        lax.all_gather(mixing_weight, "dp", axis=1, tiled=True),
        lax.all_gather(output_weight, "dp", axis=1, tiled=True),
        lax.all_gather(up_weight, "dp", axis=0, tiled=True),
        lax.all_gather(down_weight, "dp", axis=1, tiled=True),
    )
    row_count = inputs.shape[0]
    images = row_count // SEQ
    width = mixing_full.shape[2]
    split_shape = (images, SEQ, width // HD, HD)
    scale = HD ** (-0.5)
    source = inputs.astype(jnp.float32)
    normed_one, inverse_one, affine_one = norm_forward(source, first_gain, first_shift)
    mixed_in = affine_one.astype(jnp.bfloat16)
    projected = jnp.einsum("nd,jde->jne", mixed_in, mixing_full, preferred_element_type=jnp.float32)
    query = (projected[0] + attend_bias[0]).astype(jnp.bfloat16).reshape(split_shape)
    keys = projected[1].astype(jnp.bfloat16).reshape(split_shape)
    values = (projected[2] + attend_bias[1]).astype(jnp.bfloat16).reshape(split_shape)
    scores = jnp.einsum("bqhd,bkhd->bhqk", query, keys, preferred_element_type=jnp.float32) * scale
    top = jnp.max(scores, axis=-1, keepdims=True)
    logsum = top + jnp.log(jnp.sum(jnp.exp(scores - top), axis=-1, keepdims=True))
    probs = jnp.exp(scores - logsum).astype(jnp.bfloat16)
    attended = (
        jnp.einsum("bhqk,bkhd->bqhd", probs, values, preferred_element_type=jnp.float32)
        .astype(jnp.bfloat16)
        .reshape(row_count, width)
    )
    residual = source + lax.psum(matmul(attended, output_full), "tensor") + output_bias
    normed_two, inverse_two, affine_two = norm_forward(residual, second_gain, second_shift)
    hidden_in = affine_two.astype(jnp.bfloat16)
    preact = matmul(hidden_in, up_full) + hidden_bias
    active_full, slope = gelu_pair(preact)
    active = active_full.astype(jnp.bfloat16)
    layer_output = (residual + lax.psum(matmul(active, down_full), "tensor") + final_bias).astype(
        jnp.bfloat16
    )
    mixing_back, output_back, up_back, down_back = (mixing_full, output_full, up_full, down_full)
    upstream = cotangent.astype(jnp.float32)
    down_grad = matmul(active.T, cotangent)
    finalbias_grad = jnp.sum(upstream, axis=0)
    pre_grad = matmul(cotangent, down_back.T) * slope
    pre_half = pre_grad.astype(jnp.bfloat16)
    up_grad = matmul(hidden_in.T, pre_half)
    hiddenbias_grad = jnp.sum(pre_grad, axis=0)
    affine_two_grad = lax.psum(matmul(pre_half, up_back.T), "tensor")
    secondgain_grad = jnp.sum(affine_two_grad * normed_two, axis=0)
    secondshift_grad = jnp.sum(affine_two_grad, axis=0)
    residual_grad = upstream + norm_backward(affine_two_grad, normed_two, inverse_two, second_gain)
    residual_half = residual_grad.astype(jnp.bfloat16)
    outweight_grad = matmul(attended.T, residual_half)
    outbias_grad = jnp.sum(residual_grad, axis=0)
    attended_grad = matmul(residual_half, output_back.T).astype(jnp.bfloat16).reshape(split_shape)
    recomputed = (
        jnp.einsum("bqhd,bkhd->bhqk", query, keys, preferred_element_type=jnp.float32) * scale
    )
    probs_full = jnp.exp(recomputed - logsum)
    prob_grad = jnp.einsum(
        "bqhd,bkhd->bhqk", attended_grad, values, preferred_element_type=jnp.float32
    )
    delta = jnp.sum(probs_full * prob_grad, axis=-1, keepdims=True)
    score_grad = (probs_full * (prob_grad - delta) * scale).astype(jnp.bfloat16)
    query_grad = jnp.einsum(
        "bhqk,bkhd->bqhd", score_grad, keys, preferred_element_type=jnp.float32
    ).reshape(row_count, width)
    keys_grad = jnp.einsum(
        "bhqk,bqhd->bkhd", score_grad, query, preferred_element_type=jnp.float32
    ).reshape(row_count, width)
    values_grad = jnp.einsum(
        "bhqk,bqhd->bkhd", probs, attended_grad, preferred_element_type=jnp.float32
    ).reshape(row_count, width)
    attendbias_grad = jnp.stack([jnp.sum(query_grad, axis=0), jnp.sum(values_grad, axis=0)])
    stacked = jnp.stack([query_grad, keys_grad, values_grad]).astype(jnp.bfloat16)
    mixing_grad = jnp.einsum("nd,jne->jde", mixed_in, stacked, preferred_element_type=jnp.float32)
    affine_one_grad = lax.psum(
        jnp.einsum("jne,jde->nd", stacked, mixing_back, preferred_element_type=jnp.float32),
        "tensor",
    )
    firstgain_grad = jnp.sum(affine_one_grad * normed_one, axis=0)
    firstshift_grad = jnp.sum(affine_one_grad, axis=0)
    input_grad = (
        residual_grad + norm_backward(affine_one_grad, normed_one, inverse_one, first_gain)
    ).astype(jnp.bfloat16)
    mixing_share, output_share, up_share, down_share = (
        lax.psum_scatter(mixing_grad, "dp", scatter_dimension=1, tiled=True),
        lax.psum_scatter(outweight_grad, "dp", scatter_dimension=1, tiled=True),
        lax.psum_scatter(up_grad, "dp", scatter_dimension=0, tiled=True),
        lax.psum_scatter(down_grad, "dp", scatter_dimension=1, tiled=True),
    )
    vector_totals = lax.psum(
        (
            firstgain_grad,
            firstshift_grad,
            attendbias_grad,
            outbias_grad,
            hiddenbias_grad,
            finalbias_grad,
            secondgain_grad,
            secondshift_grad,
        ),
        "dp",
    )
    return (
        layer_output,
        input_grad,
        mixing_share,
        output_share,
        up_share,
        down_share,
        vector_totals[0],
        vector_totals[1],
        vector_totals[2],
        vector_totals[3],
        vector_totals[4],
        vector_totals[5],
        vector_totals[6],
        vector_totals[7],
    )


ROWS = 256
SENT = 208
X = 2
C = 2
TILE = 384
SCALE = HD ** (-0.5)
F32 = jnp.float32
BF16 = jnp.bfloat16


def nt(left, right):
    return lax.dot_general(left, right, (((1,), (1,)), ((), ())), preferred_element_type=F32)


def tn(left, right):
    return lax.dot_general(left, right, (((0,), (0,)), ((), ())), preferred_element_type=F32)


def cols(tile):
    return pl.ds(pl.multiple_of(tile * TILE, TILE), TILE)


def layer_kernel(
    Z,
    copies,
    x_ref,
    ct_ref,
    mix_ref,
    outw_ref,
    up_ref,
    down_ref,
    fg_ref,
    fs_ref,
    ab_ref,
    ob_ref,
    hb_ref,
    fb_ref,
    sg_ref,
    ss_ref,
    lo_ref,
    ig_ref,
    gmix_ref,
    gout_ref,
    gup_ref,
    gdown_ref,
    vec_ref,
    w0,
    w1,
    w2,
    w3,
    g0,
    g1,
    g2,
    g3,
    ga0,
    ga1,
    ga2,
    ga3,
    gb0,
    gb1,
    gb2,
    gb3,
    gc0,
    gc1,
    gc2,
    gc3,
    gd0,
    gd1,
    gd2,
    gd3,
    ge0,
    ge1,
    ge2,
    ge3,
    ysend,
    yrecv,
    vs,
    vr,
    left_t,
    n1_s,
    n2_s,
    acc,
    qkv,
    prob_s,
    att,
    attg,
    stacked,
    active,
    slope,
    pre_half,
    a2_s,
    res_s,
    rg_s,
    ct_s,
    rows_s,
    send_sem,
    recv_sem,
):
    dp = lax.axis_index("dp")
    tensor = lax.axis_index("tensor")
    c = lax.rem(dp, C)
    x = lax.rem(dp // C, X)
    z = dp // (C * X)
    w = (w0, w1, w2, w3)
    g = (g0, g1, g2, g3)
    ga = (ga0, ga1, ga2, ga3)
    gb = (gb0, gb1, gb2, gb3)
    gc = (gc0, gc1, gc2, gc3)
    gd = (gd0, gd1, gd2, gd3)
    ge = (ge0, ge1, ge2, ge3)

    def index(zz, xx, cc):
        return (zz * X + xx) * C + cc

    def zat(step):
        return lax.rem(z + step + Z, Z)

    peers_z = [{"dp": index(zat(d), x, c), "tensor": tensor} for d in range(1, Z)]
    peer_x = {"dp": index(z, 1 - x, c), "tensor": tensor}
    peer_c = {"dp": index(z, x, 1 - c), "tensor": tensor}
    peer_y = {"dp": dp, "tensor": 1 - tensor}

    started = []

    def send(src, dst, device):
        k = len(started)
        copy = pltpu.make_async_remote_copy(
            src_ref=src,
            dst_ref=dst,
            send_sem=send_sem.at[k],
            recv_sem=recv_sem.at[k],
            device_id=device,
            device_id_type=pl.DeviceIdType.MESH,
        )
        copy.start()
        started.append(copy)
        return copy

    yrecv[:, SENT:ROWS, :] = jnp.zeros((4, ROWS - SENT, yrecv.shape[2]), BF16)
    for j in range(3):
        w0[z, x, c, :, j * TILE : (j + 1) * TILE] = mix_ref[j]
    w1[z, x, c] = outw_ref[...]
    w2[z, x, c] = up_ref[...]
    w3[z, x, c] = down_ref[...]

    barrier = pltpu.get_barrier_semaphore()
    everyone = peers_z + [peer_x, peer_c, peer_y]
    for device in everyone:
        pl.semaphore_signal(barrier, inc=1, device_id=device, device_id_type=pl.DeviceIdType.MESH)
    pl.semaphore_wait(barrier, len(everyone))

    by_z, by_x, by_c, by_d = {}, {}, {}, {}

    def own(i):
        mine = w[i].at[z, x, c]
        by_x[i, 0] = send(mine, mine, peer_x)
        for d in range(1, Z):
            by_z[i, d] = send(mine, mine, peers_z[d - 1])
        by_c[i, 0] = send(mine, mine, peer_c)

    own(0)
    own(1)

    def pass_on(i):
        for d in range(1, Z):
            by_z[i, d].wait_recv()
            block = w[i].at[zat(-d), x, c]
            by_x[i, d] = send(block, block, peer_x)
            by_c[i, d] = send(block, block, peer_c)

    def pass_core(i):
        for d in range(Z):
            by_x[i, d].wait_recv()
            block = w[i].at[zat(-d), 1 - x, c]
            by_d[i, d] = send(block, block, peer_c)

    def gathered(i):
        for d in range(Z):
            by_c[i, d].wait_recv()
        for d in range(Z):
            by_d[i, d].wait_recv()

    def weight(i, tile):
        return w[i][:, :, :, :, cols(tile)].reshape(-1, TILE)

    def exchange(k):
        return send(ysend.at[k, pl.ds(0, SENT)], yrecv.at[k, pl.ds(0, SENT)], peer_y)

    def exchanged(k):
        return ysend[k].astype(F32) + yrecv[k].astype(F32)

    def transposed(value):
        return value.astype(F32).T.astype(BF16)

    rg_s[192:ROWS, :] = jnp.zeros((ROWS - 192, rg_s.shape[1]), F32)
    rg_s[0:SEQ, :] = x_ref[...].astype(F32)
    acc[192:ROWS, :] = jnp.zeros((ROWS - 192, acc.shape[1]), F32)
    acc[0:SEQ, :] = ct_ref[...].astype(F32)
    ct_s[...] = acc[...].astype(BF16)
    for row, ref in enumerate((fg_ref, fs_ref, ob_ref, fb_ref, sg_ref)):
        rows_s[row : row + 1, 0:768] = ref[...].reshape(1, -1)
    rows_s[0:1, 768:1536] = ss_ref[...].reshape(1, -1)
    rows_s[5:6, :] = hb_ref[...].reshape(1, -1)
    fg_row, fs_row, ob_row, fb_row, sg_row = (rows_s.at[r : r + 1, 0:768] for r in range(5))
    ss_row = rows_s.at[0:1, 768:1536]
    source = rg_s[...]
    n1, r1, affine = norm_forward(source, fg_row[...], fs_row[...])
    n1_s[...] = n1
    a1 = affine.astype(BF16)
    left_t[0] = transposed(a1)
    left_t[1] = transposed(ct_s[...])
    vs[...] = jnp.zeros_like(vs)
    vs[6:7, :] = jnp.sum(ct_s[...].astype(F32), axis=0, keepdims=True)
    pass_on(0)
    own(2)
    pass_core(0)
    pass_on(1)
    own(3)
    gathered(0)

    for j in range(3):
        value = jnp.dot(a1, weight(0, j), preferred_element_type=F32)
        if j != 1:
            value = value + ab_ref[j // 2 : j // 2 + 1, :]
        qkv[:, j * TILE : (j + 1) * TILE] = value.astype(BF16)
    pass_core(1)

    heads = TILE // HD
    seen = lax.broadcasted_iota(jnp.int32, (ROWS, ROWS), 1) < SEQ

    def head(ref, part, h):
        pair = ref[:, part * TILE + (h // 2) * 128 : part * TILE + (h // 2) * 128 + 128]
        return pair[:, (h % 2) * HD : (h % 2) * HD + HD]

    halves = []
    for h in range(heads):
        q, k, v = head(qkv, 0, h), head(qkv, 1, h), head(qkv, 2, h)
        scores = jnp.where(seen, nt(q, k) * SCALE, -1e30)
        top = jnp.max(scores, axis=-1, keepdims=True)
        logsum = top + jnp.log(jnp.sum(jnp.exp(scores - top), axis=-1, keepdims=True))
        probs = jnp.exp(scores - logsum)
        prob_s[h] = probs
        halves.append(jnp.dot(probs.astype(BF16), v, preferred_element_type=F32))
        if h % 2 == 1:
            att[:, (h // 2) * 128 : (h // 2) * 128 + 128] = jnp.concatenate(
                halves[-2:], axis=1
            ).astype(BF16)
        if h == 1:
            pass_on(2)
    gathered(1)
    ysend[0] = nt(att[...], weight(1, 0)).astype(BF16)
    first = exchange(0)
    pass_core(2)
    pass_on(3)
    first.wait_recv()
    residual = source + exchanged(0) + ob_row[...]
    res_s[...] = residual
    n2, r2, affine = norm_forward(residual, sg_row[...], ss_row[...])
    n2_s[...] = n2
    a2_s[...] = affine.astype(BF16)
    left_t[2] = transposed(affine.astype(BF16))
    gathered(2)
    tiles = hb_ref.shape[0] // TILE

    def hidden(tile, carry):
        value = jnp.dot(a2_s[...], weight(2, tile), preferred_element_type=F32)
        value, steep = gelu_pair(value + rows_s[5:6, cols(tile)])
        active[:, cols(tile)] = value.astype(BF16)
        slope[:, cols(tile)] = steep
        return carry

    lax.fori_loop(0, tiles, hidden, 0)
    pass_core(3)
    by_a, by_b, by_e = {}, {}, {}

    def gradient(i, left, right, count):
        def one(tile, carry):
            value = jnp.dot(left_t[left], right[:, cols(tile)], preferred_element_type=F32)
            g[i][:, :, :, :, cols(tile)] = value.astype(BF16).reshape(Z, X, C, -1, TILE)
            return carry

        lax.fori_loop(0, count, one, 0)
        by_a[i] = send(g[i].at[:, :, 1 - c], ga[i], peer_c)

    def sum_core(i):
        by_a[i].wait_recv()
        gb[i][...] = (g[i][:, :, c].astype(F32) + ga[i][...].astype(F32)).astype(BF16)
        by_b[i] = send(gb[i].at[:, 1 - x], gc[i], peer_x)

    def sum_x(i):
        by_b[i].wait_recv()
        gd[i][...] = (gb[i][:, x].astype(F32) + gc[i][...].astype(F32)).astype(BF16)
        for d in range(1, Z):
            by_e[i, d] = send(gd[i].at[zat(d)], ge[i].at[d], peers_z[d - 1])

    def sum_z(i):
        total = gd[i][z].astype(F32)
        for d in range(1, Z):
            by_e[i, d].wait_recv()
            total = total + ge[i][d].astype(F32)
        return total

    gradient(3, 1, active, tiles)
    gathered(3)

    acc[...] = jnp.zeros_like(acc)

    def second(tile, carry):
        acc[...] += nt(active[:, cols(tile)], weight(3, tile))
        return carry

    lax.fori_loop(0, tiles, second, 0)
    ysend[1] = acc[...].astype(BF16)
    out_copy = exchange(1)
    sum_core(3)

    acc[...] = jnp.zeros_like(acc)

    def back(tile, carry):
        grad = jnp.dot(ct_s[...], weight(3, tile), preferred_element_type=F32)
        grad = grad * slope[:, cols(tile)]
        sums = jnp.sum(grad, axis=0, keepdims=True)
        slope[0:8, cols(tile)] = jnp.broadcast_to(sums, (8, TILE))
        half = grad.astype(BF16)
        pre_half[:, cols(tile)] = half
        acc[...] += nt(half, weight(2, tile))
        return carry

    lax.fori_loop(0, tiles, back, 0)
    ysend[2] = acc[...].astype(BF16)
    a2_copy = exchange(2)
    vs[4:5, :] = slope[0:1, 0:768]
    vs[5:6, :] = slope[0:1, 768:1536]

    gradient(2, 2, pre_half, tiles)
    out_copy.wait_recv()
    lo_ref[...] = (res_s[...] + exchanged(1) + fb_row[...]).astype(BF16)
    a2_copy.wait_recv()
    a2_grad = exchanged(2)
    vs[7:8, :] = jnp.sum(a2_grad * n2_s[...], axis=0, keepdims=True)
    vs[8:9, :] = jnp.sum(a2_grad, axis=0, keepdims=True)
    res_grad = ct_s[...].astype(F32) + norm_backward(a2_grad, n2_s[...], r2, sg_row[...])
    rg_s[...] = res_grad
    vs[3:4, :] = jnp.sum(res_grad, axis=0, keepdims=True)
    res_half = res_grad.astype(BF16)
    left_t[1] = transposed(res_half)
    sum_core(2)
    sum_x(3)
    attg[...] = jnp.dot(res_half, weight(1, 0), preferred_element_type=F32).astype(BF16)
    gradient(1, 1, att, 1)

    pairs = {}
    for h in range(heads):
        q, k, v = head(qkv, 0, h), head(qkv, 1, h), head(qkv, 2, h)
        upper = head(attg, 0, h)
        probs = prob_s[h]
        prob_grad = nt(upper, v)
        delta = jnp.sum(probs * prob_grad, axis=-1, keepdims=True)
        score_grad = (probs * (prob_grad - delta) * SCALE).astype(BF16)
        pairs[0, h] = jnp.dot(score_grad, k, preferred_element_type=F32)
        pairs[1, h] = tn(score_grad, q)
        pairs[2, h] = tn(probs.astype(BF16), upper)
        if h % 2 == 1:
            start = (h // 2) * 128
            for j in range(3):
                pair = jnp.concatenate([pairs[j, h - 1], pairs[j, h]], axis=1)
                stacked[:, j * TILE + start : j * TILE + start + 128] = pair.astype(BF16)
                if j != 1:
                    place = (j // 2) * TILE + start
                    vs[2:3, place : place + 128] = jnp.sum(pair, axis=0, keepdims=True)
        if h == 1:
            sum_core(1)
        if h == 3:
            sum_x(2)
    gradient(0, 0, stacked, 3)
    total = nt(stacked[:, 0:TILE], weight(0, 0))
    for j in range(1, 3):
        total = total + nt(stacked[:, j * TILE : (j + 1) * TILE], weight(0, j))
    ysend[3] = total.astype(BF16)
    last = exchange(3)
    sum_core(0)
    sum_x(1)
    last.wait_recv()
    a1_grad = exchanged(3)
    vs[0:1, :] = jnp.sum(a1_grad * n1_s[...], axis=0, keepdims=True)
    vs[1:2, :] = jnp.sum(a1_grad, axis=0, keepdims=True)
    vec_c = send(vs, vr.at[0], peer_c)
    ig_ref[...] = (rg_s[...] + norm_backward(a1_grad, n1_s[...], r1, fg_row[...])).astype(BF16)
    vec_c.wait_recv()
    vr[1] = vs[...] + vr[0]
    vec_x = send(vr.at[1], vr.at[2], peer_x)
    gdown_ref[...] = sum_z(3)
    gup_ref[...] = sum_z(2)
    vec_x.wait_recv()
    mine = vr[1] + vr[2]
    vr[3 + z] = mine
    vec_z = [send(vr.at[3 + z], vr.at[3 + z], peers_z[d - 1]) for d in range(1, Z)]
    sum_x(0)
    gout_ref[...] = sum_z(1)
    for copy in vec_z:
        copy.wait_recv()
    total = vr[3]
    for d in range(1, Z):
        total = total + vr[3 + d]
    vec_ref[...] = total
    total = sum_z(0)
    for j in range(3):
        gmix_ref[j] = total[:, j * TILE : (j + 1) * TILE]
    for copy in started:
        copy.wait_send()
    assert len(started) == copies


def local(sizes, *arrays):
    n = sizes["dp"]
    inputs, mixing, up = arrays[0], arrays[2], arrays[4]
    shard = mixing.shape[1]
    fits = (
        shard % 16 == 0
        and n % (X * C) == 0
        and sizes["tensor"] == 2
        and inputs.shape == (SEQ, 768)
        and mixing.shape[2] == TILE
        and up.shape[1] == 1536
    )
    if not fits:
        return local_plain(*arrays)
    (
        inputs,
        cotangent,
        mixing,
        output,
        up,
        down,
        first_gain,
        first_shift,
        attend_bias,
        output_bias,
        hidden_bias,
        final_bias,
        second_gain,
        second_shift,
    ) = arrays
    Z = n // (X * C)
    width = inputs.shape[1]
    sizes_of = (3 * TILE, TILE, up.shape[1], up.shape[1])
    copies = 4 * (Z - 1 + 3 * Z) + 4 + 4 * (Z + 1) + Z + 1
    vmem = pl.BlockSpec(memory_space=pltpu.VMEM)
    full = [pltpu.VMEM((Z, X, C, shard, k), BF16) for k in sizes_of]
    half = [pltpu.VMEM((Z, X, shard, k), BF16) for k in sizes_of]
    quarter = [pltpu.VMEM((Z, shard, k), BF16) for k in sizes_of]
    outs = pl.pallas_call(
        functools.partial(layer_kernel, Z, copies),
        out_shape=(
            jax.ShapeDtypeStruct((ROWS, width), BF16),
            jax.ShapeDtypeStruct((ROWS, width), BF16),
            jax.ShapeDtypeStruct((3, shard, TILE), F32),
            jax.ShapeDtypeStruct((shard, TILE), F32),
            jax.ShapeDtypeStruct((shard, up.shape[1]), F32),
            jax.ShapeDtypeStruct((shard, up.shape[1]), F32),
            jax.ShapeDtypeStruct((16, width), F32),
        ),
        in_specs=[vmem] * 14,
        out_specs=(vmem,) * 7,
        scratch_shapes=full
        + full
        + half
        + half
        + quarter
        + quarter
        + quarter
        + [
            pltpu.VMEM((4, ROWS, width), BF16),
            pltpu.VMEM((4, ROWS, width), BF16),
            pltpu.VMEM((16, width), F32),
            pltpu.VMEM((3 + Z, 16, width), F32),
            pltpu.VMEM((3, width, ROWS), BF16),
            pltpu.VMEM((ROWS, width), F32),
            pltpu.VMEM((ROWS, width), F32),
            pltpu.VMEM((ROWS, width), F32),
            pltpu.VMEM((ROWS, 3 * TILE), BF16),
            pltpu.VMEM((TILE // HD, ROWS, ROWS), F32),
            pltpu.VMEM((ROWS, TILE), BF16),
            pltpu.VMEM((ROWS, TILE), BF16),
            pltpu.VMEM((ROWS, 3 * TILE), BF16),
            pltpu.VMEM((ROWS, up.shape[1]), BF16),
            pltpu.VMEM((ROWS, up.shape[1]), F32),
            pltpu.VMEM((ROWS, up.shape[1]), BF16),
            pltpu.VMEM((ROWS, width), BF16),
            pltpu.VMEM((ROWS, width), F32),
            pltpu.VMEM((ROWS, width), F32),
            pltpu.VMEM((ROWS, width), BF16),
            pltpu.VMEM((6, up.shape[1]), F32),
            pltpu.SemaphoreType.DMA((copies,)),
            pltpu.SemaphoreType.DMA((copies,)),
        ],
        compiler_params=pltpu.CompilerParams(
            collective_id=0, has_side_effects=True, vmem_limit_bytes=60 * 1024 * 1024
        ),
    )(
        inputs,
        cotangent,
        mixing,
        output.T,
        up,
        down.T,
        first_gain,
        first_shift,
        attend_bias,
        output_bias,
        hidden_bias,
        final_bias,
        second_gain,
        second_shift,
    )
    layer_output, input_grad, gmix, gout, gup, gdown, vec = outs
    return (
        layer_output[:SEQ],
        input_grad[:SEQ],
        gmix,
        gout.T,
        gup,
        gdown.T,
        vec[0],
        vec[1],
        vec[2].reshape(2, TILE),
        vec[3],
        vec[4:6].reshape(-1),
        vec[6],
        vec[7],
        vec[8],
    )


def solution(mesh):
    placed = (
        P("dp", None),
        P("dp", None),
        P(None, "dp", "tensor"),
        P("tensor", "dp"),
        P("dp", "tensor"),
        P("tensor", "dp"),
        P(),
        P(),
        P(None, "tensor"),
        P(),
        P("tensor"),
        P(),
        P(),
        P(),
    )
    return jax.shard_map(
        functools.partial(local, dict(mesh.shape)),
        mesh=mesh,
        in_specs=placed,
        out_specs=(
            P("dp", None),
            P("dp", None),
            P(None, "dp", "tensor"),
            P("tensor", "dp"),
            P("dp", "tensor"),
            P("tensor", "dp"),
            P(),
            P(),
            P(None, "tensor"),
            P(),
            P("tensor"),
            P(),
            P(),
            P(),
        ),
        check_vma=False,
    )
```
